32 devices in a mesh: segment: 4 (over y, x), dp: 8 (over z, core).
Axes of the slice: x: 2, y: 2, z: 4, core: 2. Of those that a mesh axis runs over, the one named last changes fastest.
Arguments:
- images: bfloat16 [32, 16, 16, 512], P('dp'), may hold values from -6 to 6
- labels: int32 [32], P('dp'), may hold values from 0 to 999
- counts: int32 [4], replicated, may hold values from 1 to 4, as said below
- depthwise: bfloat16 [16, 9, 512], P('segment'), may hold values from -2 to 2
- pointwise: bfloat16 [16, 512, 512], P('segment'), may hold values from -0.09375 to 0.09375
- head_weight: float32 [512, 1000], replicated, may hold values from -0.25 to 0.25
Outputs:
- grad_pointwise: float32 [16, 512, 512], P('segment', 'dp')
- grad_depthwise: float32 [16, 9, 512], P('segment', None, 'dp')
The draws below stay inside these ranges and needn't reach their ends.
Inputs may be any that keep to these rules, and one draw needn't show every extreme that they name: Section s runs its first counts[s] cell slots; some section runs all 4 and another a single cell.
All inputs are finite; a program needn't handle non-finite values.
Results may differ from the reference program's by a relative error of at most 0.00085.
Values may be sent and summed in bfloat16 or wider, within the bound.
A program may use at most 128 MiB of HBM per device.

```python
import jax
import jax.numpy as jnp
from jax import lax

CHAN = 512
CLASSES = 1000
SIDE = 16
CELLS = 4
MICRO = 4
BATCH_MB = 1
IMAGES = 32
SLOTS = 16
N_SEGMENT = 4
N_DP = 8


def draw_counts(key, part):
    first_key = jax.random.fold_in(key, 11)
    second_key = jax.random.fold_in(key, 23)
    values = jax.random.randint(first_key, (N_SEGMENT,), 1, CELLS + 1)
    fullest = jax.random.randint(second_key, (), 0, N_SEGMENT)
    segments = jnp.arange(N_SEGMENT, dtype=jnp.int32)
    values = jnp.where(segments == fullest, CELLS, values)
    values = jnp.where(segments == (fullest + 1) % N_SEGMENT, 1, values)
    return values.astype(jnp.int32)


def touch_ends(values, rng, smallest, largest):
    index_at = [jax.random.randint(jax.random.fold_in(rng, axis), (), 0, length) for axis, length in enumerate(values.shape)]
    widest = values.shape.index(max(values.shape))
    neighbour = index_at[:widest] + [(index_at[widest] + 1) % values.shape[widest]] + index_at[widest + 1:]
    return values.at[tuple(index_at)].set(smallest).at[tuple(neighbour)].set(largest)


def level_of(own_key, dims, shards, least, top_value):
    gain = 1.0
    for position, parts in shards:
        heights = jax.random.uniform(jax.random.fold_in(jax.random.fold_in(own_key, 6), position), (parts,), jnp.float32, least / len(shards), top_value / len(shards))
        gain = gain * jnp.repeat(jnp.exp(heights), dims[position] // parts).reshape((-1,) + (1,) * (len(dims) - 1 - position))
    return gain


def noise(own_key, shape, deviation, reach, pieces=(), kind=jnp.bfloat16):
    factor_of = level_of(own_key, shape, pieces, -0.22, 0.18) if pieces else 1.0
    entries = jax.random.normal(own_key, shape, jnp.float32) * deviation * factor_of
    return jnp.minimum(jnp.maximum(entries, -reach), reach).astype(kind)


def setup_inputs(seed: int = 0) -> dict:
    arg_keys = jax.random.split(jax.random.key(seed), 7)
    return {
        "images": noise(arg_keys[0], (IMAGES, SIDE, SIDE, CHAN), 1.0, 6.0, ((0, 8),)),
        "labels": touch_ends(jax.random.randint(arg_keys[1], (IMAGES,), 0, CLASSES), jax.random.fold_in(arg_keys[1], 1), 0, CLASSES - 1).astype(jnp.int32),
        "counts": draw_counts(jax.random.fold_in(arg_keys[6], 71), 0),
        "depthwise": noise(arg_keys[3], (SLOTS, 9, CHAN), 9 ** -0.5, 2.0, ((0, 4),)),
        "pointwise": noise(arg_keys[4], (SLOTS, CHAN, CHAN), (8 * CHAN) ** -0.5, 0.09375, ((0, 4),)),
        "head_weight": noise(arg_keys[5], (CHAN, CLASSES), CHAN ** -0.5, 0.25, (), jnp.float32),
    }


def offsets(dilation):
    return [(row * dilation, col * dilation) for row in (-1, 0, 1) for col in (-1, 0, 1)]

def shifted_view(field, shift_row, shift_col):
    side = field.shape[1]
    padded = jnp.pad(field, ((0, 0), (2, 2), (2, 2), (0, 0)))
    return padded[:, 2 + shift_row:2 + shift_row + side, 2 + shift_col:2 + shift_col + side, :]

def depth_mix(relu_field, kernel, dilation):
    kernel_wide = kernel.astype(jnp.float32)
    mixed = jnp.zeros(relu_field.shape, jnp.float32)
    for tap_index, (shift_row, shift_col) in enumerate(offsets(dilation)):
        mixed = mixed + shifted_view(relu_field, shift_row, shift_col).astype(jnp.float32) * kernel_wide[tap_index]
    return mixed.astype(jnp.bfloat16)

def cell_forward(field, kernel, weight, dilation):
    relu_field = jnp.maximum(field, jnp.zeros((), field.dtype))
    spread = depth_mix(relu_field, kernel, dilation)
    width = field.shape[3]
    projected = jnp.dot(spread.reshape(-1, width), weight, preferred_element_type=jnp.float32).reshape(field.shape)
    return (field.astype(jnp.float32) + projected).astype(jnp.bfloat16)

def cell_backward(field, cotangent, kernel, weight, dilation):
    width = field.shape[3]
    relu_field = jnp.maximum(field, jnp.zeros((), field.dtype))
    spread = depth_mix(relu_field, kernel, dilation)
    flat_grad = cotangent.reshape(-1, width)
    grad_weight = lax.dot_general(spread.reshape(-1, width), flat_grad, (((0,), (0,)), ((), ())), preferred_element_type=jnp.float32)
    grad_spread = lax.dot_general(flat_grad, weight, (((1,), (1,)), ((), ())), preferred_element_type=jnp.float32)
    spread_wide = grad_spread.astype(jnp.bfloat16).reshape(field.shape).astype(jnp.float32)
    kernel_wide = kernel.astype(jnp.float32)
    kernel_rows = []
    back_sum = jnp.zeros(field.shape, jnp.float32)
    for tap_index, (shift_row, shift_col) in enumerate(offsets(dilation)):
        kernel_rows.append(lax.optimization_barrier(jnp.sum(spread_wide * shifted_view(relu_field, shift_row, shift_col).astype(jnp.float32), axis=(0, 1, 2))))
        back_sum = back_sum + shifted_view(spread_wide, -shift_row, -shift_col) * kernel_wide[tap_index]
    grad_kernel = jnp.stack(kernel_rows)
    grad_in = (cotangent.astype(jnp.float32) + jnp.where(field > 0, back_sum, jnp.zeros((), jnp.float32))).astype(jnp.bfloat16)
    return (grad_in, grad_weight, grad_kernel)

def head_grad(final, head_weight, label_row, image_total):
    pooled = lax.optimization_barrier(jnp.mean(final.astype(jnp.float32), axis=(1, 2)))
    logits = jnp.dot(pooled, head_weight, precision=lax.Precision.HIGHEST, preferred_element_type=jnp.float32)
    classes = jnp.arange(head_weight.shape[1], dtype=jnp.int32)
    target = (label_row[:, None] == classes[None, :]).astype(jnp.float32)
    error_term = (jax.nn.sigmoid(logits) - target) / image_total
    back_pool = jnp.dot(error_term, head_weight.T, precision=lax.Precision.HIGHEST, preferred_element_type=jnp.float32)
    back_pool = back_pool / (final.shape[1] * final.shape[2])
    return jnp.broadcast_to(back_pool[:, None, None, :], final.shape).astype(jnp.bfloat16)

def reference(images, labels, counts, depthwise, pointwise, head_weight):
    slot_total = depthwise.shape[0]
    per_segment = slot_total // N_SEGMENT
    image_total = N_DP * MICRO * BATCH_MB
    batches = images.reshape(N_DP * MICRO, BATCH_MB, SIDE, SIDE, CHAN)
    label_rows = labels.reshape(N_DP * MICRO, BATCH_MB)
    live_slots = [counts[slot // per_segment] > slot % per_segment for slot in range(slot_total)]

    def one_micro(running, micro_item):
        weight_sums, kernel_sums = running
        field, label_row = micro_item
        inputs = []
        for slot in range(slot_total):
            inputs.append(field)
            result = cell_forward(field, depthwise[slot], pointwise[slot], 1 + slot % per_segment % 2)
            field = jnp.where(live_slots[slot], result, field)
        cotangent = head_grad(field, head_weight, label_row, image_total)
        weight_list = [None] * slot_total
        kernel_list = [None] * slot_total
        for slot in reversed(range(slot_total)):
            grad_in, grad_weight, grad_kernel = cell_backward(inputs[slot], cotangent, depthwise[slot], pointwise[slot], 1 + slot % per_segment % 2)
            weight_list[slot] = jnp.where(live_slots[slot], grad_weight, jnp.zeros((), jnp.float32))
            kernel_list[slot] = jnp.where(live_slots[slot], grad_kernel, jnp.zeros((), jnp.float32))
            cotangent = jnp.where(live_slots[slot], grad_in, cotangent)
        return ((weight_sums + jnp.stack(weight_list), kernel_sums + jnp.stack(kernel_list)), None)
    zeros_init = (jnp.zeros(pointwise.shape, jnp.float32), jnp.zeros(depthwise.shape, jnp.float32))
    (weight_sums, kernel_sums), unused = lax.scan(one_micro, zeros_init, (batches, label_rows))
    return (weight_sums, kernel_sums)
```

```python
import functools

import jax
import jax.numpy as jnp
from jax import lax
from jax.experimental import pallas as pl
from jax.experimental.pallas import tpu as pltpu
from jax.sharding import PartitionSpec as P

LANES = 128
PAD = 2


def span(start, size):
    return pl.ds(pl.multiple_of(start, size), size)


def kernel(
    micros, slots, sections, side, image_total,
    images, target, depthwise, pointwise, pointwise_t, head_weight, live,
    grad_weight, grad_kernel,
    fields, spreads, cots, relu_pad, grad_pad, taps_acc, pooled,
    send_fwd, recv_fwd, send_bwd, recv_bwd,
):
    area = side * side
    width = images.shape[-1]
    here = lax.axis_index("segment")
    last = sections - 1
    chunks = [slice(c, c + LANES) for c in range(0, width, LANES)]

    def ahead(m):
        return pltpu.make_async_remote_copy(
            src_ref=fields.at[span((slots * micros + m) * area, area)],
            dst_ref=fields.at[span(m * area, area)],
            send_sem=send_fwd.at[m],
            recv_sem=recv_fwd.at[m],
            device_id={"segment": here + 1},
            device_id_type=pl.DeviceIdType.MESH,
        )

    def behind(m):
        return pltpu.make_async_remote_copy(
            src_ref=cots.at[span(m * area, area)],
            dst_ref=cots.at[span((slots * micros + m) * area, area)],
            send_sem=send_bwd.at[m],
            recv_sem=recv_bwd.at[m],
            device_id={"segment": here - 1},
            device_id_type=pl.DeviceIdType.MESH,
        )

    barrier = pltpu.get_barrier_semaphore()

    @pl.when(here > 0)
    def _():
        pl.semaphore_signal(
            barrier, inc=1, device_id={"segment": here - 1}, device_id_type=pl.DeviceIdType.MESH
        )

    @pl.when(here < last)
    def _():
        pl.semaphore_signal(
            barrier, inc=1, device_id={"segment": here + 1}, device_id_type=pl.DeviceIdType.MESH
        )

    inner_section = (here > 0) & (here < last)

    @pl.when(inner_section)
    def _():
        pl.semaphore_wait(barrier, 2)

    @pl.when(jnp.logical_not(inner_section))
    def _():
        pl.semaphore_wait(barrier, 1)

    edge = PAD * side
    for ref in (relu_pad, grad_pad.at[0], grad_pad.at[1], grad_pad.at[2]):
        ref[0:edge] = jnp.zeros((edge, width), jnp.float32)
        ref[edge + area : 2 * edge + area] = jnp.zeros((edge, width), jnp.float32)
    taps_acc[...] = jnp.zeros_like(taps_acc)
    cols = lax.broadcasted_iota(jnp.int32, (side, LANES), 0)

    def moved(value, shift):
        rolled = pltpu.roll(value, shift % side, 0)
        keep = cols >= shift if shift > 0 else cols < side + shift
        return jnp.where(keep, rolled, 0.0)

    def forward_cell(m, j, dilation):
        base = (j * micros + m) * area
        kernels = depthwise[j]
        relu_pad[edge : edge + area] = jnp.maximum(
            fields[span(base, area)].astype(jnp.float32), 0.0
        )
        for lanes in chunks:
            taps = [
                jnp.broadcast_to(kernels[t : t + 1, lanes], (side, LANES)) for t in range(9)
            ]

            def row_step(quad, carry):
                for extra in range(4):
                    row = quad * 4 + extra
                    rows = [
                        relu_pad[span((row + PAD + a * dilation) * side, side), lanes]
                        for a in (-1, 0, 1)
                    ]
                    parts = [
                        rows[0] * taps[b] + rows[1] * taps[3 + b] + rows[2] * taps[6 + b]
                        for b in range(3)
                    ]
                    total = parts[1] + moved(parts[0], dilation) + moved(parts[2], -dilation)
                    spreads[span(base + row * side, side), lanes] = total.astype(jnp.bfloat16)
                return carry

            lax.fori_loop(0, side // 4, row_step, 0)
        fields[span(base + micros * area, area)] = (
            fields[span(base, area)].astype(jnp.float32)
            + jnp.dot(
                spreads[span(base, area)], pointwise[j], preferred_element_type=jnp.float32
            )
        ).astype(jnp.bfloat16)

    def backward_cell(m, j, dilation):
        base = (j * micros + m) * area
        above = base + micros * area
        kernels = depthwise[j]
        grad_pad[1, edge : edge + area] = (
            jnp.dot(cots[span(above, area)], pointwise_t[j], preferred_element_type=jnp.float32)
            .astype(jnp.bfloat16)
            .astype(jnp.float32)
        )
        for lanes in chunks:
            taps = [
                jnp.broadcast_to(kernels[t : t + 1, lanes], (side, LANES)) for t in range(9)
            ]

            def shift_step(quad, carry):
                for extra in range(4):
                    at = span((quad * 4 + extra + PAD) * side, side)
                    value = grad_pad[1, at, lanes]
                    grad_pad[0, at, lanes] = moved(value, -dilation)
                    grad_pad[2, at, lanes] = moved(value, dilation)
                return carry

            lax.fori_loop(0, side // 4, shift_step, 0)

            def row_step(pair, sums):
                sums = list(sums)
                for extra in range(2):
                    row = pair * 2 + extra
                    field = fields[span(base + row * side, side), lanes].astype(jnp.float32)
                    relu = jnp.maximum(field, 0.0)
                    back = jnp.zeros((side, LANES), jnp.float32)
                    for t in range(9):
                        a, b = t // 3 - 1, t % 3
                        piece = grad_pad[
                            b, span((row + PAD - a * dilation) * side, side), lanes
                        ]
                        back = back + piece * taps[t]
                        term = piece * relu
                        sums[t] = sums[t] + (term[0:8] + term[8:16])
                    cot = cots[span(above + row * side, side), lanes].astype(jnp.float32)
                    cots[span(base + row * side, side), lanes] = (
                        cot + jnp.where(field > 0.0, back, 0.0)
                    ).astype(jnp.bfloat16)
                return tuple(sums)

            start = tuple(taps_acc[j, 8 * t : 8 * t + 8, lanes] for t in range(9))
            done = lax.fori_loop(0, side // 2, row_step, start)
            for t in range(9):
                taps_acc[j, 8 * t : 8 * t + 8, lanes] = done[t]

    def forward_micro(m, carry):
        @pl.when(here == 0)
        def _():
            fields[span(m * area, area)] = images[span(m * area, area)]

        @pl.when(here > 0)
        def _():
            ahead(m).wait_recv()

        def pair_step(pair, inner):
            for parity in range(2):
                forward_cell(m, pair * 2 + parity, 1 + parity)
            return inner

        lax.fori_loop(0, slots // 2, pair_step, 0)

        @pl.when(here < last)
        def _():
            ahead(m).start()

        return carry

    lax.fori_loop(0, micros, forward_micro, 0)

    @pl.when(here == last)
    def _():
        pooled[...] = jnp.zeros_like(pooled)
        for m in range(micros):
            final = fields[(slots * micros + m) * area : (slots * micros + m + 1) * area]
            pooled[m : m + 1] = jnp.sum(
                final.astype(jnp.float32), axis=0, keepdims=True
            ) * (1.0 / area)
        logits = jnp.dot(
            pooled[...],
            head_weight[...],
            precision=lax.Precision.HIGHEST,
            preferred_element_type=jnp.float32,
        )
        error_term = (1.0 / (1.0 + jnp.exp(-logits)) - target[...]) / image_total
        back = lax.dot_general(
            error_term,
            head_weight[...],
            (((1,), (1,)), ((), ())),
            precision=lax.Precision.HIGHEST,
            preferred_element_type=jnp.float32,
        ) / area
        for m in range(micros):
            cots[(slots * micros + m) * area : (slots * micros + m + 1) * area] = (
                jnp.broadcast_to(back[m : m + 1], (area, width)).astype(jnp.bfloat16)
            )

    def backward_micro(m, carry):
        @pl.when(here < last)
        def _():
            behind(m).wait_recv()

        def pair_step(pair, inner):
            for parity in (1, 0):
                backward_cell(m, slots - 2 - pair * 2 + parity, 1 + parity)
            return inner

        lax.fori_loop(0, slots // 2, pair_step, 0)

        @pl.when(here > 0)
        def _():
            behind(m).start()

        return carry

    lax.fori_loop(0, micros, backward_micro, 0)

    def finish(j, carry):
        rows = micros * area
        grad_weight[j] = (
            lax.dot_general(
                spreads[span(j * rows, rows)],
                cots[span((j + 1) * rows, rows)],
                (((0,), (0,)), ((), ())),
                preferred_element_type=jnp.float32,
            )
            * live[j, 0:1]
        )
        return carry

    lax.fori_loop(0, slots, finish, 0)
    for j in range(slots):
        for t in range(9):
            grad_kernel[j, t : t + 1] = jnp.sum(
                taps_acc[j, 8 * t : 8 * t + 8], axis=0, keepdims=True
            )

    @pl.when(here < last)
    def _():
        for m in range(micros):
            ahead(m).wait_send()

    @pl.when(here > 0)
    def _():
        for m in range(micros):
            behind(m).wait_send()


def local(images, labels, counts, depthwise, pointwise, head_weight):
    slots, _, width = depthwise.shape
    micros, side = images.shape[:2]
    area = side * side
    sections = lax.axis_size("segment")
    replicas = lax.axis_size("dp")
    here = lax.axis_index("segment")
    image_total = micros * replicas
    classes = head_weight.shape[1]
    classes_pad = -(-classes // LANES) * LANES
    count_here = jnp.sum(
        jnp.where(jnp.arange(sections, dtype=jnp.int32) == here, counts, 0)
    )
    live = jnp.arange(slots, dtype=jnp.int32) < count_here
    weight = jnp.where(live[:, None, None], pointwise, jnp.zeros((), pointwise.dtype))
    weight_t = jnp.swapaxes(weight, 1, 2)
    live_rows = jnp.broadcast_to(live.astype(jnp.float32)[:, None, None], (slots, 8, width))
    target = (labels[:, None] == jnp.arange(classes_pad, dtype=jnp.int32)[None, :]).astype(
        jnp.float32
    )
    target = jnp.pad(target, ((0, 8 - micros), (0, 0)))
    head = jnp.pad(head_weight, ((0, 0), (0, classes_pad - classes)))
    vmem = pl.BlockSpec(memory_space=pltpu.VMEM)
    padded = area + 2 * PAD * side
    grad_weight, grad_kernel = pl.pallas_call(
        functools.partial(kernel, micros, slots, sections, side, image_total),
        out_shape=(
            jax.ShapeDtypeStruct((slots, width, width), jnp.float32),
            jax.ShapeDtypeStruct((slots, 9, width), jnp.float32),
        ),
        in_specs=[vmem] * 7,
        out_specs=(vmem, vmem),
        scratch_shapes=[
            pltpu.VMEM(((slots + 1) * micros * area, width), jnp.bfloat16),
            pltpu.VMEM((slots * micros * area, width), jnp.bfloat16),
            pltpu.VMEM(((slots + 1) * micros * area, width), jnp.bfloat16),
            pltpu.VMEM((padded, width), jnp.float32),
            pltpu.VMEM((3, padded, width), jnp.float32),
            pltpu.VMEM((slots, 72, width), jnp.float32),
            pltpu.VMEM((8, width), jnp.float32),
            pltpu.SemaphoreType.DMA((micros,)),
            pltpu.SemaphoreType.DMA((micros,)),
            pltpu.SemaphoreType.DMA((micros,)),
            pltpu.SemaphoreType.DMA((micros,)),
        ],
        compiler_params=pltpu.CompilerParams(
            collective_id=0, has_side_effects=True, vmem_limit_bytes=52 * 1024 * 1024
        ),
    )(
        images.reshape(micros * area, width),
        target,
        depthwise.astype(jnp.float32),
        weight,
        weight_t,
        head,
        live_rows,
    )
    part = width // replicas
    rest = grad_kernel.reshape(slots, 9, replicas, part).swapaxes(1, 2)
    rest = rest.reshape(slots, replicas, 9 * part)
    rest = jnp.pad(rest, ((0, 0), (0, 0), (0, 8 * width - 9 * part)))
    rest = rest.reshape(slots, replicas, 8, width)
    packed = jnp.concatenate([grad_weight.reshape(slots, replicas, part, width), rest], axis=2)
    packed = packed.reshape(slots, replicas * (part + 8), width)
    summed = lax.psum_scatter(packed, "dp", scatter_dimension=1, tiled=True)
    return (
        summed[:, :part],
        summed[:, part:].reshape(slots, 8 * width)[:, : 9 * part].reshape(slots, 9, part),
    )


def solution(mesh):
    in_specs = (
        P("dp", None, None, None),
        P("dp"),
        P(),
        P("segment", None, None),
        P("segment", None, None),
        P(),
    )
    out_specs = (P("segment", "dp", None), P("segment", None, "dp"))
    return jax.shard_map(local, mesh=mesh, in_specs=in_specs, out_specs=out_specs, check_vma=False)
```

```python
import functools

import jax
import jax.numpy as jnp
from jax import lax
from jax.experimental import pallas as pl
from jax.experimental.pallas import tpu as pltpu
from jax.sharding import PartitionSpec as P

LANES = 128
PAD = 2


def span(start, size):
    return pl.ds(pl.multiple_of(start, size), size)


def kernel(
    micros, slots, sections, chips, side, image_total,
    labels, counts, images, depthwise, pointwise, head_weight,
    grad_weight, grad_kernel,
    fields, spreads, cots, relu_pad, grad_pad, taps_acc, pooled, pointwise_t,
    whole, twin, rise, fall, whole_k, twin_k, rise_k, fall_k,
    send_fwd, recv_fwd, send_bwd, recv_bwd,
    send_twin, recv_twin, send_rise, recv_rise, send_fall, recv_fall,
):
    area = side * side
    width = images.shape[-1]
    here = lax.axis_index("segment")
    last = sections - 1
    chunks = [slice(c, c + LANES) for c in range(0, width, LANES)]

    def ahead(m):
        return pltpu.make_async_remote_copy(
            src_ref=fields.at[span((slots * micros + m) * area, area)],
            dst_ref=fields.at[span(m * area, area)],
            send_sem=send_fwd.at[m],
            recv_sem=recv_fwd.at[m],
            device_id={"segment": here + 1},
            device_id_type=pl.DeviceIdType.MESH,
        )

    def behind(m):
        return pltpu.make_async_remote_copy(
            src_ref=cots.at[span(m * area, area)],
            dst_ref=cots.at[span((slots * micros + m) * area, area)],
            send_sem=send_bwd.at[m],
            recv_sem=recv_bwd.at[m],
            device_id={"segment": here - 1},
            device_id_type=pl.DeviceIdType.MESH,
        )

    replica = lax.axis_index("dp")
    chip, core = lax.div(replica, 2), lax.rem(replica, 2)
    part = grad_weight.shape[1]

    def to_twin(j):
        if j is None:
            src, dst, at = whole_k, twin_k, slots
        else:
            src, dst, at = whole.at[j, :, 1 - core], twin.at[j], j
        return pltpu.make_async_remote_copy(
            src_ref=src, dst_ref=dst, send_sem=send_twin.at[at], recv_sem=recv_twin.at[at],
            device_id={"dp": replica + 1 - 2 * core}, device_id_type=pl.DeviceIdType.MESH,
        )

    def up(j, k):
        ref, at = (rise_k.at[k], slots) if j is None else (rise.at[j, k], j)
        return pltpu.make_async_remote_copy(
            src_ref=ref, dst_ref=ref, send_sem=send_rise.at[at, k], recv_sem=recv_rise.at[at, k],
            device_id={"dp": replica + 2}, device_id_type=pl.DeviceIdType.MESH,
        )

    def down(j, k):
        ref, at = (fall_k.at[k], slots) if j is None else (fall.at[j, k], j)
        return pltpu.make_async_remote_copy(
            src_ref=ref, dst_ref=ref, send_sem=send_fall.at[at, k], recv_sem=recv_fall.at[at, k],
            device_id={"dp": replica - 2}, device_id_type=pl.DeviceIdType.MESH,
        )

    def own(j, k):
        if j is None:
            return whole_k[k] + twin_k[k]
        return whole[j, k, core] + twin[j, k]

    barrier = pltpu.get_barrier_semaphore()

    def greet(where, target):
        @pl.when(where)
        def _():
            pl.semaphore_signal(
                barrier, inc=1, device_id=target, device_id_type=pl.DeviceIdType.MESH
            )

        return jnp.where(where, 1, 0).astype(jnp.int32)

    peers = greet(here > 0, {"segment": here - 1})
    peers += greet(here < last, {"segment": here + 1})
    peers += greet(chip > 0, {"dp": replica - 2})
    peers += greet(chip < chips - 1, {"dp": replica + 2})
    pl.semaphore_signal(
        barrier, inc=1, device_id={"dp": replica + 1 - 2 * core},
        device_id_type=pl.DeviceIdType.MESH,
    )
    pl.semaphore_wait(barrier, peers + 1)
    count_here = counts[here]

    def live(j):
        return jnp.where(j < count_here, 1.0, 0.0)

    def turn_weights():
        for j in range(slots):
            pointwise_t[j] = jnp.swapaxes(pointwise[j], 0, 1)

    edge = PAD * side
    for ref in (relu_pad, grad_pad.at[0], grad_pad.at[1], grad_pad.at[2]):
        ref[0:edge] = jnp.zeros((edge, width), jnp.float32)
        ref[edge + area : 2 * edge + area] = jnp.zeros((edge, width), jnp.float32)
    taps_acc[...] = jnp.zeros_like(taps_acc)
    cols = lax.broadcasted_iota(jnp.int32, (side, LANES), 0)

    def moved(value, shift):
        rolled = pltpu.roll(value, shift % side, 0)
        keep = cols >= shift if shift > 0 else cols < side + shift
        return jnp.where(keep, rolled, 0.0)

    def forward_cell(m, j, dilation):
        base = (j * micros + m) * area
        kernels = depthwise[j].astype(jnp.float32)
        relu_pad[edge : edge + area] = jnp.maximum(
            fields[span(base, area)].astype(jnp.float32), 0.0
        )
        for lanes in chunks:
            taps = [
                jnp.broadcast_to(kernels[t : t + 1, lanes], (side, LANES)) for t in range(9)
            ]

            def row_step(quad, carry):
                for extra in range(4):
                    row = quad * 4 + extra
                    rows = [
                        relu_pad[span((row + PAD + a * dilation) * side, side), lanes]
                        for a in (-1, 0, 1)
                    ]
                    parts = [
                        rows[0] * taps[b] + rows[1] * taps[3 + b] + rows[2] * taps[6 + b]
                        for b in range(3)
                    ]
                    total = parts[1] + moved(parts[0], dilation) + moved(parts[2], -dilation)
                    spreads[span(base + row * side, side), lanes] = total.astype(jnp.bfloat16)
                return carry

            lax.fori_loop(0, side // 4, row_step, 0)
        fields[span(base + micros * area, area)] = (
            fields[span(base, area)].astype(jnp.float32)
            + jnp.dot(
                spreads[span(base, area)], pointwise[j], preferred_element_type=jnp.float32
            )
            * live(j)
        ).astype(jnp.bfloat16)

    def backward_cell(m, j, dilation):
        base = (j * micros + m) * area
        above = base + micros * area
        kernels = depthwise[j].astype(jnp.float32)
        grad_pad[1, edge : edge + area] = (
            (
                jnp.dot(
                    cots[span(above, area)], pointwise_t[j], preferred_element_type=jnp.float32
                )
                * live(j)
            )
            .astype(jnp.bfloat16)
            .astype(jnp.float32)
        )
        for lanes in chunks:
            taps = [
                jnp.broadcast_to(kernels[t : t + 1, lanes], (side, LANES)) for t in range(9)
            ]

            def shift_step(quad, carry):
                for extra in range(4):
                    at = span((quad * 4 + extra + PAD) * side, side)
                    value = grad_pad[1, at, lanes]
                    grad_pad[0, at, lanes] = moved(value, -dilation)
                    grad_pad[2, at, lanes] = moved(value, dilation)
                return carry

            lax.fori_loop(0, side // 4, shift_step, 0)

            def row_step(pair, sums):
                sums = list(sums)
                for extra in range(2):
                    row = pair * 2 + extra
                    field = fields[span(base + row * side, side), lanes].astype(jnp.float32)
                    relu = jnp.maximum(field, 0.0)
                    back = jnp.zeros((side, LANES), jnp.float32)
                    for t in range(9):
                        a, b = t // 3 - 1, t % 3
                        piece = grad_pad[
                            b, span((row + PAD - a * dilation) * side, side), lanes
                        ]
                        back = back + piece * taps[t]
                        term = piece * relu
                        sums[t] = sums[t] + (term[0:8] + term[8:16])
                    cot = cots[span(above + row * side, side), lanes].astype(jnp.float32)
                    cots[span(base + row * side, side), lanes] = (
                        cot + jnp.where(field > 0.0, back, 0.0)
                    ).astype(jnp.bfloat16)
                return tuple(sums)

            start = tuple(taps_acc[j, 8 * t : 8 * t + 8, lanes] for t in range(9))
            done = lax.fori_loop(0, side // 2, row_step, start)
            for t in range(9):
                taps_acc[j, 8 * t : 8 * t + 8, lanes] = done[t]

    def forward_micro(m, carry):
        @pl.when(here == 0)
        def _():
            fields[span(m * area, area)] = images[m].reshape(area, width)

        @pl.when(here > 0)
        def _():
            ahead(m).wait_recv()

        def pair_step(pair, inner):
            for parity in range(2):
                forward_cell(m, pair * 2 + parity, 1 + parity)
            return inner

        lax.fori_loop(0, slots // 2, pair_step, 0)

        @pl.when(here < last)
        def _():
            ahead(m).start()

        return carry

    pl.when(here == last)(turn_weights)
    lax.fori_loop(0, micros, forward_micro, 0)
    pl.when(here < last)(turn_weights)

    @pl.when(here == last)
    def _():
        pooled[...] = jnp.zeros_like(pooled)
        for m in range(micros):
            final = fields[(slots * micros + m) * area : (slots * micros + m + 1) * area]
            pooled[m : m + 1] = jnp.sum(
                final.astype(jnp.float32), axis=0, keepdims=True
            ) * (1.0 / area)
        logits = jnp.dot(
            pooled[...],
            head_weight[...],
            precision=lax.Precision.HIGHEST,
            preferred_element_type=jnp.float32,
        )
        classes = lax.broadcasted_iota(jnp.int32, logits.shape, 1)
        image = lax.broadcasted_iota(jnp.int32, logits.shape, 0)
        target = jnp.zeros(logits.shape, jnp.float32)
        for m in range(micros):
            target += jnp.where((image == m) & (classes == labels[m]), 1.0, 0.0)
        error_term = (1.0 / (1.0 + jnp.exp(-logits)) - target) / image_total
        back = lax.dot_general(
            error_term,
            head_weight[...],
            (((1,), (1,)), ((), ())),
            precision=lax.Precision.HIGHEST,
            preferred_element_type=jnp.float32,
        ) / area
        for m in range(micros):
            cots[(slots * micros + m) * area : (slots * micros + m + 1) * area] = (
                jnp.broadcast_to(back[m : m + 1], (area, width)).astype(jnp.bfloat16)
            )

    def backward_micro(m, carry):
        @pl.when(here < last)
        def _():
            behind(m).wait_recv()

        def pair_step(pair, inner):
            for parity in (1, 0):
                backward_cell(m, slots - 2 - pair * 2 + parity, 1 + parity)
            return inner

        lax.fori_loop(0, slots // 2, pair_step, 0)

        @pl.when(here > 0)
        def _():
            behind(m).start()

        return carry

    lax.fori_loop(0, micros, backward_micro, 0)

    def finish(j, carry):
        rows = micros * area
        total = (
            lax.dot_general(
                spreads[span(j * rows, rows)],
                cots[span((j + 1) * rows, rows)],
                (((0,), (0,)), ((), ())),
                preferred_element_type=jnp.float32,
            )
            * live(j)
        )
        whole[j] = total.reshape(chips, 2, part, width)
        to_twin(j).start()
        return carry

    lax.fori_loop(0, slots, finish, 0)
    whole_k[...] = jnp.zeros_like(whole_k)
    for j in range(slots):
        for t in range(9):
            tap_sum = jnp.sum(taps_acc[j, 8 * t : 8 * t + 8], axis=0, keepdims=True)
            for k in range(chips):
                lane = 2 * part * k // LANES * LANES
                whole_k[k, 16 * j + t : 16 * j + t + 1] = tap_sum[:, lane : lane + LANES]
    to_twin(None).start()

    def relay(j):
        rising, falling = (rise_k, fall_k) if j is None else (rise.at[j], fall.at[j])

        def block_step(i, carry):
            k_up, k_down = chips - 1 - i, i

            @pl.when(k_up > chip)
            def _():
                @pl.when(chip == 0)
                def _():
                    rising[k_up] = own(j, k_up)

                @pl.when(chip > 0)
                def _():
                    up(j, k_up).wait_recv()
                    rising[k_up] = rising[k_up] + own(j, k_up)

                up(j, k_up).start()

            @pl.when(k_down < chip)
            def _():
                @pl.when(chip == chips - 1)
                def _():
                    falling[k_down] = own(j, k_down)

                @pl.when(chip < chips - 1)
                def _():
                    down(j, k_down).wait_recv()
                    falling[k_down] = falling[k_down] + own(j, k_down)

                down(j, k_down).start()

            return carry

        to_twin(j).wait_recv()
        lax.fori_loop(0, chips - 1, block_step, 0)

    def settle(j):
        rising, falling = (rise_k, fall_k) if j is None else (rise.at[j], fall.at[j])
        out = grad_kernel if j is None else grad_weight.at[j]
        out[...] = own(j, chip)

        @pl.when(chip > 0)
        def _():
            up(j, chip).wait_recv()
            out[...] = out[...] + rising[chip]

        @pl.when(chip < chips - 1)
        def _():
            down(j, chip).wait_recv()
            out[...] = out[...] + falling[chip]

    def sent(j):
        def block_step(k, carry):
            @pl.when(k > chip)
            def _():
                up(j, k).wait_send()

            @pl.when(k < chip)
            def _():
                down(j, k).wait_send()

            return carry

        to_twin(j).wait_send()
        lax.fori_loop(0, chips, block_step, 0)

    for step in (relay, settle, sent):
        def slot_step(j, carry, step=step):
            step(j)
            return carry

        lax.fori_loop(0, slots, slot_step, 0)
        step(None)

    @pl.when(here < last)
    def _():
        for m in range(micros):
            ahead(m).wait_send()

    @pl.when(here > 0)
    def _():
        for m in range(micros):
            behind(m).wait_send()


def local(images, labels, counts, depthwise, pointwise, head_weight):
    slots, _, width = depthwise.shape
    micros, side = images.shape[:2]
    area = side * side
    sections = lax.axis_size("segment")
    replicas = lax.axis_size("dp")
    chips = replicas // 2
    part = width // replicas
    vmem = pl.BlockSpec(memory_space=pltpu.VMEM)
    smem = pl.BlockSpec(memory_space=pltpu.SMEM)
    padded = area + 2 * PAD * side
    blocks = pltpu.VMEM((slots, chips, part, width), jnp.float32)
    blocks_k = pltpu.VMEM((chips, slots * 16, LANES), jnp.float32)
    grad_weight, grad_kernel = pl.pallas_call(
        functools.partial(kernel, micros, slots, sections, chips, side, micros * replicas),
        out_shape=(
            jax.ShapeDtypeStruct((slots, part, width), jnp.float32),
            jax.ShapeDtypeStruct((slots * 16, LANES), jnp.float32),
        ),
        in_specs=[smem] * 2 + [vmem] * 4,
        out_specs=(vmem, vmem),
        scratch_shapes=[
            pltpu.VMEM(((slots + 1) * micros * area, width), jnp.bfloat16),
            pltpu.VMEM((slots * micros * area, width), jnp.bfloat16),
            pltpu.VMEM(((slots + 1) * micros * area, width), jnp.bfloat16),
            pltpu.VMEM((padded, width), jnp.float32),
            pltpu.VMEM((3, padded, width), jnp.float32),
            pltpu.VMEM((slots, 72, width), jnp.float32),
            pltpu.VMEM((8, width), jnp.float32),
            pltpu.VMEM((slots, width, width), jnp.bfloat16),
            pltpu.VMEM((slots, chips, 2, part, width), jnp.float32),
            blocks, blocks, blocks,
            blocks_k, blocks_k, blocks_k, blocks_k,
        ]
        + [pltpu.SemaphoreType.DMA((micros,))] * 4
        + [pltpu.SemaphoreType.DMA((slots + 1,))] * 2
        + [pltpu.SemaphoreType.DMA((slots + 1, chips))] * 4,
        compiler_params=pltpu.CompilerParams(
            collective_id=0, has_side_effects=True, vmem_limit_bytes=56 * 1024 * 1024
        ),
    )(labels, counts, images, depthwise, pointwise, head_weight)
    lane = lax.rem(lax.axis_index("dp") * part, LANES)
    mine = lax.dynamic_slice_in_dim(grad_kernel, lane, part, 1)
    return grad_weight, mine.reshape(slots, 16, part)[:, :9]


def solution(mesh):
    in_specs = (
        P("dp", None, None, None),
        P("dp"),
        P(),
        P("segment", None, None),
        P("segment", None, None),
        P(),
    )
    out_specs = (P("segment", "dp", None), P("segment", None, "dp"))
    return jax.shard_map(local, mesh=mesh, in_specs=in_specs, out_specs=out_specs, check_vma=False)
```

```python
import functools

import jax
import jax.numpy as jnp
from jax import lax
from jax.experimental import pallas as pl
from jax.experimental.pallas import tpu as pltpu
from jax.sharding import PartitionSpec as P

LANES = 128
PAD = 2


def span(start, size):
    return pl.ds(pl.multiple_of(start, size), size)


def kernel(
    micros, slots, sections, chips, side, image_total,
    labels, counts, images, depthwise, pointwise, head_weight,
    grad_weight, grad_kernel,
    fields, spreads, cots, relu_pad, grad_pad, taps_acc, pooled, pointwise_t, tap_rows,
    whole, twin, rise, fall, whole_k, twin_k, rise_k, fall_k,
    send_fwd, recv_fwd, send_bwd, recv_bwd,
    send_twin, recv_twin, send_rise, recv_rise, send_fall, recv_fall,
):
    area = side * side
    width = images.shape[-1]
    here = lax.axis_index("segment")
    last = sections - 1
    chunks = [slice(c, c + LANES) for c in range(0, width, LANES)]

    def ahead(m):
        return pltpu.make_async_remote_copy(
            src_ref=fields.at[span((slots * micros + m) * area, area)],
            dst_ref=fields.at[span(m * area, area)],
            send_sem=send_fwd.at[m],
            recv_sem=recv_fwd.at[m],
            device_id={"segment": here + 1},
            device_id_type=pl.DeviceIdType.MESH,
        )

    def behind(m):
        return pltpu.make_async_remote_copy(
            src_ref=cots.at[span(m * area, area)],
            dst_ref=cots.at[span((slots * micros + m) * area, area)],
            send_sem=send_bwd.at[m],
            recv_sem=recv_bwd.at[m],
            device_id={"segment": here - 1},
            device_id_type=pl.DeviceIdType.MESH,
        )

    replica = lax.axis_index("dp")
    chip, core = lax.div(replica, 2), lax.rem(replica, 2)
    part = grad_weight.shape[1]

    def to_twin(j):
        if j is None:
            src, dst, at = whole_k, twin_k, slots
        else:
            src, dst, at = whole.at[j, :, 1 - core], twin.at[j], j
        return pltpu.make_async_remote_copy(
            src_ref=src, dst_ref=dst, send_sem=send_twin.at[at], recv_sem=recv_twin.at[at],
            device_id={"dp": replica + 1 - 2 * core}, device_id_type=pl.DeviceIdType.MESH,
        )

    def up(j, k):
        ref, at = (rise_k.at[k], slots) if j is None else (rise.at[j, k], j)
        return pltpu.make_async_remote_copy(
            src_ref=ref, dst_ref=ref, send_sem=send_rise.at[at, k], recv_sem=recv_rise.at[at, k],
            device_id={"dp": replica + 2}, device_id_type=pl.DeviceIdType.MESH,
        )

    def down(j, k):
        ref, at = (fall_k.at[k], slots) if j is None else (fall.at[j, k], j)
        return pltpu.make_async_remote_copy(
            src_ref=ref, dst_ref=ref, send_sem=send_fall.at[at, k], recv_sem=recv_fall.at[at, k],
            device_id={"dp": replica - 2}, device_id_type=pl.DeviceIdType.MESH,
        )

    def own(j, k):
        if j is None:
            return whole_k[k] + twin_k[k]
        return whole[j, k, core] + twin[j, k]

    barrier = pltpu.get_barrier_semaphore()

    def greet(where, target):
        @pl.when(where)
        def _():
            pl.semaphore_signal(
                barrier, inc=1, device_id=target, device_id_type=pl.DeviceIdType.MESH
            )

        return jnp.where(where, 1, 0).astype(jnp.int32)

    peers = greet(here > 0, {"segment": here - 1})
    peers += greet(here < last, {"segment": here + 1})
    peers += greet(chip > 0, {"dp": replica - 2})
    peers += greet(chip < chips - 1, {"dp": replica + 2})
    pl.semaphore_signal(
        barrier, inc=1, device_id={"dp": replica + 1 - 2 * core},
        device_id_type=pl.DeviceIdType.MESH,
    )
    pl.semaphore_wait(barrier, peers + 1)
    count_here = counts[here]

    def live(j):
        return jnp.where(j < count_here, 1.0, 0.0)

    def turn_weights():
        for j in range(slots):
            pointwise_t[j] = jnp.swapaxes(pointwise[j], 0, 1)

    edge = PAD * side
    for ref in (relu_pad, grad_pad.at[0], grad_pad.at[1], grad_pad.at[2]):
        ref[0:edge] = jnp.zeros((edge, width), jnp.float32)
        ref[edge + area : 2 * edge + area] = jnp.zeros((edge, width), jnp.float32)
    taps_acc[...] = jnp.zeros_like(taps_acc)
    for t in range(9):
        tap_values = depthwise[t].astype(jnp.float32)
        for j in range(slots):
            tap_rows[j, t : t + 1] = tap_values[j : j + 1]
    cols = lax.broadcasted_iota(jnp.int32, (side, LANES), 0)

    def moved(value, shift):
        rolled = pltpu.roll(value, shift % side, 0)
        keep = cols >= shift if shift > 0 else cols < side + shift
        return jnp.where(keep, rolled, 0.0)

    def forward_cell(m, j, dilation):
        base = (j * micros + m) * area
        kernels = tap_rows[j]
        relu_pad[edge : edge + area] = jnp.maximum(
            fields[span(base, area)].astype(jnp.float32), 0.0
        )
        for lanes in chunks:
            taps = [
                jnp.broadcast_to(kernels[t : t + 1, lanes], (side, LANES)) for t in range(9)
            ]

            def row_step(quad, carry):
                for extra in range(4):
                    row = quad * 4 + extra
                    rows = [
                        relu_pad[span((row + PAD + a * dilation) * side, side), lanes]
                        for a in (-1, 0, 1)
                    ]
                    parts = [
                        rows[0] * taps[b] + rows[1] * taps[3 + b] + rows[2] * taps[6 + b]
                        for b in range(3)
                    ]
                    total = parts[1] + moved(parts[0], dilation) + moved(parts[2], -dilation)
                    spreads[span(base + row * side, side), lanes] = total.astype(jnp.bfloat16)
                return carry

            lax.fori_loop(0, side // 4, row_step, 0)
        fields[span(base + micros * area, area)] = (
            fields[span(base, area)].astype(jnp.float32)
            + jnp.dot(
                spreads[span(base, area)], pointwise[j], preferred_element_type=jnp.float32
            )
            * live(j)
        ).astype(jnp.bfloat16)

    def backward_cell(m, j, dilation):
        base = (j * micros + m) * area
        above = base + micros * area
        kernels = tap_rows[j]
        grad_pad[1, edge : edge + area] = (
            (
                jnp.dot(
                    cots[span(above, area)], pointwise_t[j], preferred_element_type=jnp.float32
                )
                * live(j)
            )
            .astype(jnp.bfloat16)
            .astype(jnp.float32)
        )
        for lanes in chunks:
            taps = [
                jnp.broadcast_to(kernels[t : t + 1, lanes], (side, LANES)) for t in range(9)
            ]

            def shift_step(quad, carry):
                for extra in range(4):
                    at = span((quad * 4 + extra + PAD) * side, side)
                    value = grad_pad[1, at, lanes]
                    grad_pad[0, at, lanes] = moved(value, -dilation)
                    grad_pad[2, at, lanes] = moved(value, dilation)
                return carry

            lax.fori_loop(0, side // 4, shift_step, 0)

            def row_step(pair, sums):
                sums = list(sums)
                for extra in range(2):
                    row = pair * 2 + extra
                    field = fields[span(base + row * side, side), lanes].astype(jnp.float32)
                    relu = jnp.maximum(field, 0.0)
                    back = jnp.zeros((side, LANES), jnp.float32)
                    for t in range(9):
                        a, b = t // 3 - 1, t % 3
                        piece = grad_pad[
                            b, span((row + PAD - a * dilation) * side, side), lanes
                        ]
                        back = back + piece * taps[t]
                        term = piece * relu
                        sums[t] = sums[t] + (term[0:8] + term[8:16])
                    cot = cots[span(above + row * side, side), lanes].astype(jnp.float32)
                    cots[span(base + row * side, side), lanes] = (
                        cot + jnp.where(field > 0.0, back, 0.0)
                    ).astype(jnp.bfloat16)
                return tuple(sums)

            start = tuple(taps_acc[j, 8 * t : 8 * t + 8, lanes] for t in range(9))
            done = lax.fori_loop(0, side // 2, row_step, start)
            for t in range(9):
                taps_acc[j, 8 * t : 8 * t + 8, lanes] = done[t]

    def forward_micro(m, carry):
        @pl.when(here == 0)
        def _():
            fields[span(m * area, area)] = images[m].reshape(area, width)

        @pl.when(here > 0)
        def _():
            ahead(m).wait_recv()

        def pair_step(pair, inner):
            for parity in range(2):
                forward_cell(m, pair * 2 + parity, 1 + parity)
            return inner

        lax.fori_loop(0, slots // 2, pair_step, 0)

        @pl.when(here < last)
        def _():
            ahead(m).start()

        return carry

    pl.when(here == last)(turn_weights)
    lax.fori_loop(0, micros, forward_micro, 0)
    pl.when(here < last)(turn_weights)

    @pl.when(here == last)
    def _():
        pooled[...] = jnp.zeros_like(pooled)
        for m in range(micros):
            final = fields[(slots * micros + m) * area : (slots * micros + m + 1) * area]
            pooled[m : m + 1] = jnp.sum(
                final.astype(jnp.float32), axis=0, keepdims=True
            ) * (1.0 / area)
        logits = lax.dot_general(
            pooled[...],
            head_weight[...],
            (((1,), (1,)), ((), ())),
            precision=lax.Precision.HIGHEST,
            preferred_element_type=jnp.float32,
        )
        classes = lax.broadcasted_iota(jnp.int32, logits.shape, 1)
        image = lax.broadcasted_iota(jnp.int32, logits.shape, 0)
        target = jnp.zeros(logits.shape, jnp.float32)
        for m in range(micros):
            target += jnp.where((image == m) & (classes == labels[m]), 1.0, 0.0)
        error_term = (1.0 / (1.0 + jnp.exp(-logits)) - target) / image_total
        back = jnp.dot(
            error_term,
            head_weight[...],
            precision=lax.Precision.HIGHEST,
            preferred_element_type=jnp.float32,
        ) / area
        for m in range(micros):
            cots[(slots * micros + m) * area : (slots * micros + m + 1) * area] = (
                jnp.broadcast_to(back[m : m + 1], (area, width)).astype(jnp.bfloat16)
            )

    def launch(j):
        rising, falling = (rise_k, fall_k) if j is None else (rise.at[j], fall.at[j])

        def block_step(i, carry):
            @pl.when(chip == 0)
            def _():
                rising[chips - 1 - i] = own(j, chips - 1 - i)
                up(j, chips - 1 - i).start()

            @pl.when(chip == chips - 1)
            def _():
                falling[i] = own(j, i)
                down(j, i).start()

            return carry

        to_twin(j).wait_recv()
        lax.fori_loop(0, chips - 1, block_step, 0)

    def finish(j):
        rows = micros * area
        total = (
            lax.dot_general(
                spreads[span(j * rows, rows)],
                cots[span((j + 1) * rows, rows)],
                (((0,), (0,)), ((), ())),
                preferred_element_type=jnp.float32,
            )
            * live(j)
        )
        whole[j] = total.reshape(chips, 2, part, width)
        to_twin(j).start()

        @pl.when(j < slots - 1)
        def _():
            launch(j + 1)

    def backward_micro(m, carry):
        @pl.when(here < last)
        def _():
            behind(m).wait_recv()

        def pair_step(pair, inner):
            for parity in (1, 0):
                slot = slots - 2 - pair * 2 + parity
                backward_cell(m, slot, 1 + parity)

                @pl.when((m == micros - 1) & (here == 0))
                def _(slot=slot):
                    finish(slot)

            return inner

        lax.fori_loop(0, slots // 2, pair_step, 0)

        @pl.when(here > 0)
        def _():
            behind(m).start()

        return carry

    lax.fori_loop(0, micros, backward_micro, 0)

    @pl.when(here > 0)
    def _():
        def slot_step(i, carry):
            finish(slots - 1 - i)
            return carry

        lax.fori_loop(0, slots, slot_step, 0)

    launch(0)
    whole_k[...] = jnp.zeros_like(whole_k)
    for j in range(slots):
        for t in range(9):
            tap_sum = jnp.sum(taps_acc[j, 8 * t : 8 * t + 8], axis=0, keepdims=True)
            for k in range(chips):
                lane = 2 * part * k // LANES * LANES
                whole_k[k, 16 * j + t : 16 * j + t + 1] = tap_sum[:, lane : lane + LANES]
    to_twin(None).start()
    launch(None)

    def relay(j):
        rising, falling = (rise_k, fall_k) if j is None else (rise.at[j], fall.at[j])

        def block_step(i, carry):
            k_up, k_down = chips - 1 - i, i

            @pl.when((k_up > chip) & (chip > 0))
            def _():
                up(j, k_up).wait_recv()
                rising[k_up] = rising[k_up] + own(j, k_up)
                up(j, k_up).start()

            @pl.when((k_down < chip) & (chip < chips - 1))
            def _():
                down(j, k_down).wait_recv()
                falling[k_down] = falling[k_down] + own(j, k_down)
                down(j, k_down).start()

            return carry

        lax.fori_loop(0, chips - 1, block_step, 0)

    def settle(j):
        rising, falling = (rise_k, fall_k) if j is None else (rise.at[j], fall.at[j])
        out = grad_kernel if j is None else grad_weight.at[j]
        out[...] = own(j, chip)

        @pl.when(chip > 0)
        def _():
            up(j, chip).wait_recv()
            out[...] = out[...] + rising[chip]

        @pl.when(chip < chips - 1)
        def _():
            down(j, chip).wait_recv()
            out[...] = out[...] + falling[chip]

    def sent(j):
        def block_step(k, carry):
            @pl.when(k > chip)
            def _():
                up(j, k).wait_send()

            @pl.when(k < chip)
            def _():
                down(j, k).wait_send()

            return carry

        to_twin(j).wait_send()
        lax.fori_loop(0, chips, block_step, 0)

    for step in (relay, settle, sent):
        def slot_step(j, carry, step=step):
            step(slots - 1 - j)
            return carry

        lax.fori_loop(0, slots, slot_step, 0)
        step(None)

    @pl.when(here < last)
    def _():
        for m in range(micros):
            ahead(m).wait_send()

    @pl.when(here > 0)
    def _():
        for m in range(micros):
            behind(m).wait_send()


def local(images, labels, counts, depthwise, pointwise, head_weight):
    slots, _, width = depthwise.shape
    micros, side = images.shape[:2]
    area = side * side
    sections = lax.axis_size("segment")
    replicas = lax.axis_size("dp")
    chips = replicas // 2
    part = width // replicas
    vmem = pl.BlockSpec(memory_space=pltpu.VMEM)
    smem = pl.BlockSpec(memory_space=pltpu.SMEM)
    padded = area + 2 * PAD * side
    blocks = pltpu.VMEM((slots, chips, part, width), jnp.float32)
    blocks_k = pltpu.VMEM((chips, slots * 16, LANES), jnp.float32)
    grad_weight, grad_kernel = pl.pallas_call(
        functools.partial(kernel, micros, slots, sections, chips, side, micros * replicas),
        out_shape=(
            jax.ShapeDtypeStruct((slots, part, width), jnp.float32),
            jax.ShapeDtypeStruct((slots * 16, LANES), jnp.float32),
        ),
        in_specs=[smem] * 2 + [vmem] * 4,
        out_specs=(vmem, vmem),
        scratch_shapes=[
            pltpu.VMEM(((slots + 1) * micros * area, width), jnp.bfloat16),
            pltpu.VMEM((slots * micros * area, width), jnp.bfloat16),
            pltpu.VMEM(((slots + 1) * micros * area, width), jnp.bfloat16),
            pltpu.VMEM((padded, width), jnp.float32),
            pltpu.VMEM((3, padded, width), jnp.float32),
            pltpu.VMEM((slots, 72, width), jnp.float32),
            pltpu.VMEM((8, width), jnp.float32),
            pltpu.VMEM((slots, width, width), jnp.bfloat16),
            pltpu.VMEM((slots, 16, width), jnp.float32),
            pltpu.VMEM((slots, chips, 2, part, width), jnp.float32),
            blocks, blocks, blocks,
            blocks_k, blocks_k, blocks_k, blocks_k,
        ]
        + [pltpu.SemaphoreType.DMA((micros,))] * 4
        + [pltpu.SemaphoreType.DMA((slots + 1,))] * 2
        + [pltpu.SemaphoreType.DMA((slots + 1, chips))] * 4,
        compiler_params=pltpu.CompilerParams(
            collective_id=0, has_side_effects=True, vmem_limit_bytes=56 * 1024 * 1024
        ),
    )(labels, counts, images, jnp.swapaxes(depthwise, 0, 1), pointwise, head_weight.T)
    lane = lax.rem(lax.axis_index("dp") * part, LANES)
    mine = lax.dynamic_slice_in_dim(grad_kernel, lane, part, 1)
    return grad_weight, mine.reshape(slots, 16, part)[:, :9]


def solution(mesh):
    in_specs = (
        P("dp", None, None, None),
        P("dp"),
        P(),
        P("segment", None, None),
        P("segment", None, None),
        P(),
    )
    out_specs = (P("segment", "dp", None), P("segment", None, "dp"))
    return jax.shard_map(local, mesh=mesh, in_specs=in_specs, out_specs=out_specs, check_vma=False)
```

```python
import functools

import jax
import jax.numpy as jnp
from jax import lax
from jax.experimental import pallas as pl
from jax.experimental.pallas import tpu as pltpu
from jax.sharding import PartitionSpec as P

LANES = 128
PAD = 2


def span(start, size):
    return pl.ds(pl.multiple_of(start, size), size)


def kernel(
    micros, slots, sections, chips, side, image_total,
    labels, counts, images, depthwise, pointwise, head_weight,
    grad_weight, grad_kernel,
    fields, spreads, cots, relu_pad, grad_pad, taps_acc, pooled, pointwise_t, tap_rows,
    whole, twin, rise, fall, whole_k, twin_k, rise_k, fall_k,
    send_fwd, recv_fwd, send_bwd, recv_bwd,
    send_twin, recv_twin, send_rise, recv_rise, send_fall, recv_fall,
):
    area = side * side
    width = images.shape[-1]
    here = lax.axis_index("segment")
    last = sections - 1
    chunks = [slice(c, c + LANES) for c in range(0, width, LANES)]

    def ahead(m):
        return pltpu.make_async_remote_copy(
            src_ref=fields.at[span((slots * micros + m) * area, area)],
            dst_ref=fields.at[span(m * area, area)],
            send_sem=send_fwd.at[m],
            recv_sem=recv_fwd.at[m],
            device_id={"segment": here + 1},
            device_id_type=pl.DeviceIdType.MESH,
        )

    def behind(m):
        return pltpu.make_async_remote_copy(
            src_ref=cots.at[span(m * area, area)],
            dst_ref=cots.at[span((slots * micros + m) * area, area)],
            send_sem=send_bwd.at[m],
            recv_sem=recv_bwd.at[m],
            device_id={"segment": here - 1},
            device_id_type=pl.DeviceIdType.MESH,
        )

    replica = lax.axis_index("dp")
    chip, core = lax.div(replica, 2), lax.rem(replica, 2)
    part = grad_weight.shape[1]

    def to_twin(j):
        if j is None:
            src, dst, at = whole_k, twin_k, slots
        else:
            src, dst, at = whole.at[j, :, 1 - core], twin.at[j], j
        return pltpu.make_async_remote_copy(
            src_ref=src, dst_ref=dst, send_sem=send_twin.at[at], recv_sem=recv_twin.at[at],
            device_id={"dp": replica + 1 - 2 * core}, device_id_type=pl.DeviceIdType.MESH,
        )

    def up(j, k):
        ref, at = (rise_k.at[k], slots) if j is None else (rise.at[j, k], j)
        return pltpu.make_async_remote_copy(
            src_ref=ref, dst_ref=ref, send_sem=send_rise.at[at, k], recv_sem=recv_rise.at[at, k],
            device_id={"dp": replica + 2}, device_id_type=pl.DeviceIdType.MESH,
        )

    def down(j, k):
        ref, at = (fall_k.at[k], slots) if j is None else (fall.at[j, k], j)
        return pltpu.make_async_remote_copy(
            src_ref=ref, dst_ref=ref, send_sem=send_fall.at[at, k], recv_sem=recv_fall.at[at, k],
            device_id={"dp": replica - 2}, device_id_type=pl.DeviceIdType.MESH,
        )

    def own(j, k):
        if j is None:
            return whole_k[k] + twin_k[k]
        return whole[j, k, core] + twin[j, k]

    barrier = pltpu.get_barrier_semaphore()

    def greet(where, target):
        @pl.when(where)
        def _():
            pl.semaphore_signal(
                barrier, inc=1, device_id=target, device_id_type=pl.DeviceIdType.MESH
            )

        return jnp.where(where, 1, 0).astype(jnp.int32)

    peers = greet(here > 0, {"segment": here - 1})
    peers += greet(here < last, {"segment": here + 1})
    peers += greet(chip > 0, {"dp": replica - 2})
    peers += greet(chip < chips - 1, {"dp": replica + 2})
    pl.semaphore_signal(
        barrier, inc=1, device_id={"dp": replica + 1 - 2 * core},
        device_id_type=pl.DeviceIdType.MESH,
    )
    pl.semaphore_wait(barrier, peers + 1)
    count_here = counts[here]

    def live(j):
        return jnp.where(j < count_here, 1.0, 0.0)

    def turn_weights():
        for j in range(slots):
            pointwise_t[j] = jnp.swapaxes(pointwise[j], 0, 1)

    edge = PAD * side
    for ref in (relu_pad, grad_pad.at[0], grad_pad.at[1], grad_pad.at[2]):
        ref[0:edge] = jnp.zeros((edge, width), jnp.float32)
        ref[edge + area : 2 * edge + area] = jnp.zeros((edge, width), jnp.float32)
    taps_acc[...] = jnp.zeros_like(taps_acc)
    for t in range(9):
        tap_values = depthwise[t].astype(jnp.float32)
        for j in range(slots):
            tap_rows[j, t : t + 1] = tap_values[j : j + 1]
    cols = lax.broadcasted_iota(jnp.int32, (side, LANES), 0)

    def moved(value, shift):
        rolled = pltpu.roll(value, shift % side, 0)
        keep = cols >= shift if shift > 0 else cols < side + shift
        return jnp.where(keep, rolled, 0.0)

    def forward_cell(m, j, dilation):
        base = (j * micros + m) * area
        kernels = tap_rows[j]
        relu_pad[edge : edge + area] = jnp.maximum(
            fields[span(base, area)].astype(jnp.float32), 0.0
        )
        for lanes in chunks:
            taps = [
                jnp.broadcast_to(kernels[t : t + 1, lanes], (side, LANES)) for t in range(9)
            ]

            def row_step(quad, carry):
                for extra in range(8):
                    row = quad * 8 + extra
                    rows = [
                        relu_pad[span((row + PAD + a * dilation) * side, side), lanes]
                        for a in (-1, 0, 1)
                    ]
                    parts = [
                        rows[0] * taps[b] + rows[1] * taps[3 + b] + rows[2] * taps[6 + b]
                        for b in range(3)
                    ]
                    total = parts[1] + moved(parts[0], dilation) + moved(parts[2], -dilation)
                    spreads[span(base + row * side, side), lanes] = total.astype(jnp.bfloat16)
                return carry

            lax.fori_loop(0, side // 8, row_step, 0)
        fields[span(base + micros * area, area)] = (
            fields[span(base, area)].astype(jnp.float32)
            + jnp.dot(
                spreads[span(base, area)], pointwise[j], preferred_element_type=jnp.float32
            )
            * live(j)
        ).astype(jnp.bfloat16)

    def backward_cell(m, j, dilation):
        base = (j * micros + m) * area
        above = base + micros * area
        kernels = tap_rows[j]
        grad_pad[1, edge : edge + area] = (
            (
                jnp.dot(
                    cots[span(above, area)], pointwise_t[j], preferred_element_type=jnp.float32
                )
                * live(j)
            )
            .astype(jnp.bfloat16)
            .astype(jnp.float32)
        )
        for lanes in chunks:
            taps = [
                jnp.broadcast_to(kernels[t : t + 1, lanes], (side, LANES)) for t in range(9)
            ]

            def shift_step(quad, carry):
                for extra in range(8):
                    at = span((quad * 8 + extra + PAD) * side, side)
                    value = grad_pad[1, at, lanes]
                    grad_pad[0, at, lanes] = moved(value, -dilation)
                    grad_pad[2, at, lanes] = moved(value, dilation)
                return carry

            lax.fori_loop(0, side // 8, shift_step, 0)

            def row_step(pair, sums):
                sums = list(sums)
                for extra in range(4):
                    row = pair * 4 + extra
                    field = fields[span(base + row * side, side), lanes].astype(jnp.float32)
                    relu = jnp.maximum(field, 0.0)
                    back = jnp.zeros((side, LANES), jnp.float32)
                    for t in range(9):
                        a, b = t // 3 - 1, t % 3
                        piece = grad_pad[
                            b, span((row + PAD - a * dilation) * side, side), lanes
                        ]
                        back = back + piece * taps[t]
                        term = piece * relu
                        sums[t] = sums[t] + (term[0:8] + term[8:16])
                    cot = cots[span(above + row * side, side), lanes].astype(jnp.float32)
                    cots[span(base + row * side, side), lanes] = (
                        cot + jnp.where(field > 0.0, back, 0.0)
                    ).astype(jnp.bfloat16)
                return tuple(sums)

            start = tuple(taps_acc[j, 8 * t : 8 * t + 8, lanes] for t in range(9))
            done = lax.fori_loop(0, side // 4, row_step, start)
            for t in range(9):
                taps_acc[j, 8 * t : 8 * t + 8, lanes] = done[t]

    def forward_micro(m, carry):
        @pl.when(here == 0)
        def _():
            fields[span(m * area, area)] = images[m].reshape(area, width)

        @pl.when(here > 0)
        def _():
            ahead(m).wait_recv()

        def pair_step(pair, inner):
            for parity in range(2):
                forward_cell(m, pair * 2 + parity, 1 + parity)
            return inner

        lax.fori_loop(0, slots // 2, pair_step, 0)

        @pl.when(here < last)
        def _():
            ahead(m).start()

        return carry

    pl.when(here == last)(turn_weights)
    lax.fori_loop(0, micros, forward_micro, 0)
    pl.when(here < last)(turn_weights)

    @pl.when(here == last)
    def _():
        pooled[...] = jnp.zeros_like(pooled)
        for m in range(micros):
            final = fields[(slots * micros + m) * area : (slots * micros + m + 1) * area]
            pooled[m : m + 1] = jnp.sum(
                final.astype(jnp.float32), axis=0, keepdims=True
            ) * (1.0 / area)
        logits = lax.dot_general(
            pooled[...],
            head_weight[...],
            (((1,), (1,)), ((), ())),
            precision=lax.Precision.HIGHEST,
            preferred_element_type=jnp.float32,
        )
        classes = lax.broadcasted_iota(jnp.int32, logits.shape, 1)
        image = lax.broadcasted_iota(jnp.int32, logits.shape, 0)
        target = jnp.zeros(logits.shape, jnp.float32)
        for m in range(micros):
            target += jnp.where((image == m) & (classes == labels[m]), 1.0, 0.0)
        error_term = (1.0 / (1.0 + jnp.exp(-logits)) - target) / image_total
        back = jnp.dot(
            error_term,
            head_weight[...],
            precision=lax.Precision.HIGHEST,
            preferred_element_type=jnp.float32,
        ) / area
        for m in range(micros):
            cots[(slots * micros + m) * area : (slots * micros + m + 1) * area] = (
                jnp.broadcast_to(back[m : m + 1], (area, width)).astype(jnp.bfloat16)
            )

    def launch(j):
        rising, falling = (rise_k, fall_k) if j is None else (rise.at[j], fall.at[j])

        def block_step(i, carry):
            @pl.when(chip == 0)
            def _():
                rising[chips - 1 - i] = own(j, chips - 1 - i)
                up(j, chips - 1 - i).start()

            @pl.when(chip == chips - 1)
            def _():
                falling[i] = own(j, i)
                down(j, i).start()

            return carry

        to_twin(j).wait_recv()
        lax.fori_loop(0, chips - 1, block_step, 0)

    def finish(j):
        rows = micros * area
        total = (
            lax.dot_general(
                spreads[span(j * rows, rows)],
                cots[span((j + 1) * rows, rows)],
                (((0,), (0,)), ((), ())),
                preferred_element_type=jnp.float32,
            )
            * live(j)
        )
        whole[j] = total.reshape(chips, 2, part, width)
        to_twin(j).start()

        @pl.when(j < slots - 1)
        def _():
            launch(j + 1)

    def backward_micro(m, carry):
        @pl.when(here < last)
        def _():
            behind(m).wait_recv()

        def pair_step(pair, inner):
            for parity in (1, 0):
                slot = slots - 2 - pair * 2 + parity
                backward_cell(m, slot, 1 + parity)

                @pl.when((m == micros - 1) & (here == 0))
                def _(slot=slot):
                    finish(slot)

            return inner

        lax.fori_loop(0, slots // 2, pair_step, 0)

        @pl.when(here > 0)
        def _():
            behind(m).start()

        return carry

    lax.fori_loop(0, micros, backward_micro, 0)

    @pl.when(here > 0)
    def _():
        def slot_step(i, carry):
            finish(slots - 1 - i)
            return carry

        lax.fori_loop(0, slots, slot_step, 0)

    launch(0)
    whole_k[...] = jnp.zeros_like(whole_k)
    for j in range(slots):
        for t in range(9):
            tap_sum = jnp.sum(taps_acc[j, 8 * t : 8 * t + 8], axis=0, keepdims=True)
            for k in range(chips):
                lane = 2 * part * k // LANES * LANES
                whole_k[k, 16 * j + t : 16 * j + t + 1] = tap_sum[:, lane : lane + LANES]
    to_twin(None).start()
    launch(None)

    def relay(j):
        rising, falling = (rise_k, fall_k) if j is None else (rise.at[j], fall.at[j])

        def block_step(i, carry):
            k_up, k_down = chips - 1 - i, i

            @pl.when((k_up > chip) & (chip > 0))
            def _():
                up(j, k_up).wait_recv()
                rising[k_up] = rising[k_up] + own(j, k_up)
                up(j, k_up).start()

            @pl.when((k_down < chip) & (chip < chips - 1))
            def _():
                down(j, k_down).wait_recv()
                falling[k_down] = falling[k_down] + own(j, k_down)
                down(j, k_down).start()

            return carry

        lax.fori_loop(0, chips - 1, block_step, 0)

    def settle(j):
        rising, falling = (rise_k, fall_k) if j is None else (rise.at[j], fall.at[j])
        out = grad_kernel if j is None else grad_weight.at[j]
        out[...] = own(j, chip)

        @pl.when(chip > 0)
        def _():
            up(j, chip).wait_recv()
            out[...] = out[...] + rising[chip]

        @pl.when(chip < chips - 1)
        def _():
            down(j, chip).wait_recv()
            out[...] = out[...] + falling[chip]

    def sent(j):
        def block_step(k, carry):
            @pl.when(k > chip)
            def _():
                up(j, k).wait_send()

            @pl.when(k < chip)
            def _():
                down(j, k).wait_send()

            return carry

        to_twin(j).wait_send()
        lax.fori_loop(0, chips, block_step, 0)

    for step in (relay, settle, sent):
        def slot_step(j, carry, step=step):
            step(slots - 1 - j)
            return carry

        lax.fori_loop(0, slots, slot_step, 0)
        step(None)

    @pl.when(here < last)
    def _():
        for m in range(micros):
            ahead(m).wait_send()

    @pl.when(here > 0)
    def _():
        for m in range(micros):
            behind(m).wait_send()


def local(images, labels, counts, depthwise, pointwise, head_weight):
    slots, _, width = depthwise.shape
    micros, side = images.shape[:2]
    area = side * side
    sections = lax.axis_size("segment")
    replicas = lax.axis_size("dp")
    chips = replicas // 2
    part = width // replicas
    vmem = pl.BlockSpec(memory_space=pltpu.VMEM)
    smem = pl.BlockSpec(memory_space=pltpu.SMEM)
    padded = area + 2 * PAD * side
    blocks = pltpu.VMEM((slots, chips, part, width), jnp.float32)
    blocks_k = pltpu.VMEM((chips, slots * 16, LANES), jnp.float32)
    grad_weight, grad_kernel = pl.pallas_call(
        functools.partial(kernel, micros, slots, sections, chips, side, micros * replicas),
        out_shape=(
            jax.ShapeDtypeStruct((slots, part, width), jnp.float32),
            jax.ShapeDtypeStruct((slots * 16, LANES), jnp.float32),
        ),
        in_specs=[smem] * 2 + [vmem] * 4,
        out_specs=(vmem, vmem),
        scratch_shapes=[
            pltpu.VMEM(((slots + 1) * micros * area, width), jnp.bfloat16),
            pltpu.VMEM((slots * micros * area, width), jnp.bfloat16),
            pltpu.VMEM(((slots + 1) * micros * area, width), jnp.bfloat16),
            pltpu.VMEM((padded, width), jnp.float32),
            pltpu.VMEM((3, padded, width), jnp.float32),
            pltpu.VMEM((slots, 72, width), jnp.float32),
            pltpu.VMEM((8, width), jnp.float32),
            pltpu.VMEM((slots, width, width), jnp.bfloat16),
            pltpu.VMEM((slots, 16, width), jnp.float32),
            pltpu.VMEM((slots, chips, 2, part, width), jnp.float32),
            blocks, blocks, blocks,
            blocks_k, blocks_k, blocks_k, blocks_k,
        ]
        + [pltpu.SemaphoreType.DMA((micros,))] * 4
        + [pltpu.SemaphoreType.DMA((slots + 1,))] * 2
        + [pltpu.SemaphoreType.DMA((slots + 1, chips))] * 4,
        compiler_params=pltpu.CompilerParams(
            collective_id=0, has_side_effects=True, vmem_limit_bytes=56 * 1024 * 1024
        ),
    )(labels, counts, images, jnp.swapaxes(depthwise, 0, 1), pointwise, head_weight.T)
    lane = lax.rem(lax.axis_index("dp") * part, LANES)
    mine = lax.dynamic_slice_in_dim(grad_kernel, lane, part, 1)
    return grad_weight, mine.reshape(slots, 16, part)[:, :9]


def solution(mesh):
    in_specs = (
        P("dp", None, None, None),
        P("dp"),
        P(),
        P("segment", None, None),
        P("segment", None, None),
        P(),
    )
    out_specs = (P("segment", "dp", None), P("segment", None, "dp"))
    return jax.shard_map(local, mesh=mesh, in_specs=in_specs, out_specs=out_specs, check_vma=False)
```
